256 devices in a mesh: gx: 8 (over x, y_hi), gy: 4 (over y_lo, core), gz: 8 (over z).
Axes of the slice: x: 4, y: 4 (y_hi: 2, y_lo: 2; y = y_hi * 2 + y_lo), z: 8, core: 2. Of those that a mesh axis runs over, the one named last changes fastest.
Arguments:
- seed_cotangent: bfloat16 [8, 4, 8, 112, 2048], P('gx', 'gy', 'gz'), may hold values from -6 to 6
- trace_operator: bfloat16 [8, 4, 8, 2048, 2048], P('gx', 'gy', 'gz'), may hold values from -0.125 to 0.125
- face_matrices: bfloat16 [8, 4, 8, 6, 340, 340], P('gx', 'gy', 'gz'), may hold values from -0.3125 to 0.3125
- saved_traces: bfloat16 [8, 4, 8, 3, 112, 2048], P('gx', 'gy', 'gz'), may hold values from -6 to 6
- edge_flags: int32 [8, 4, 8, 6], P('gx', 'gy', 'gz'), may hold values 0 or 1
- node_map: int32 [8, 4, 8, 6, 340], P('gx', 'gy', 'gz'), may hold values from 0 to 339, each once within a row
Outputs:
- adjoint_traces: bfloat16 [8, 4, 8, 112, 2048], P('gx', 'gy', 'gz')
- face_gradient: bfloat16 [8, 4, 8, 6, 340, 340], P('gx', 'gy', 'gz')
The draws below stay inside these ranges and needn't reach their ends.
Inputs may be any that keep to these rules, and one draw needn't show every extreme that they name: Each row node_map[.., k, :] names every face node once.
All inputs are finite; a program needn't handle non-finite values. No bound on the sum of `edge_flags` on one device may be relied on, other than what follows from the above.
Results may differ from the reference program's by a relative error of at most 0.0085.
Values may be sent and summed in bfloat16 or wider, within the bound.
No kernel may reach another device: no remote copies, remote signals or barrier semaphores. Data moves between devices by JAX's collectives and lax.ppermute only.
A program may use at most 64 MiB of HBM per device.

```python
import jax
import jax.numpy as jnp
from jax import lax

TRACE = 2048
F = 340
COLS = 112
ITERS = 3
NX = 8
NY = 4
NZ = 8


def set_ends(result, own_key, low, top_value):
    longest = result.shape.index(max(result.shape))
    spots = []
    for shift in (0, 1):
        where = [jax.random.randint(jax.random.fold_in(own_key, axis), (), 0, length) for axis, length in enumerate(result.shape)]
        where[longest] = (where[longest] + shift) % result.shape[longest]
        spots.append(tuple(where))
    return result.at[spots[0]].set(low).at[spots[1]].set(top_value)


def level_of(key, shape, split, smallest, largest):
    factor_of = 1.0
    for dim, blocks in split:
        draws = jax.random.uniform(jax.random.fold_in(jax.random.fold_in(key, 6), dim), (blocks,), jnp.float32, smallest / len(split), largest / len(split))
        factor_of = factor_of * jnp.repeat(jnp.exp(draws), shape[dim] // blocks).reshape((-1,) + (1,) * (len(shape) - 1 - dim))
    return factor_of


def scatter_about(rng, dims, deviation, bound, cuts=(), kind=jnp.bfloat16):
    level = level_of(rng, dims, cuts, -0.22, 0.18) if cuts else 1.0
    result = jax.random.normal(rng, dims, jnp.float32) * deviation * level
    return jnp.minimum(jnp.maximum(result, -bound), bound).astype(kind)


def setup_inputs(seed: int = 0) -> dict:
    seeds = jax.random.split(jax.random.key(seed), 7)
    return {
        "seed_cotangent": scatter_about(seeds[0], (NX, NY, NZ, COLS, TRACE), 1.0, 6.0, ((0, 8), (1, 4), (2, 8))),
        "trace_operator": scatter_about(seeds[1], (NX, NY, NZ, TRACE, TRACE), TRACE ** -0.5, 0.125, ((0, 8), (1, 4), (2, 8))),
        "face_matrices": scatter_about(seeds[2], (NX, NY, NZ, 6, F, F), F ** -0.5, 0.3125, ((0, 8), (1, 4), (2, 8))),
        "saved_traces": scatter_about(seeds[3], (NX, NY, NZ, ITERS, COLS, TRACE), 1.0, 6.0, ((0, 8), (1, 4), (2, 8))),
        "edge_flags": set_ends((jax.random.randint(seeds[4], (NX, NY, NZ, 6), 0, 4) < 1).astype(jnp.int32), jax.random.fold_in(seeds[4], 1), 0, 1),
        "node_map": jax.vmap(lambda own: jax.random.permutation(own, F))(jax.random.split(seeds[5], NX * NY * NZ * 6)).reshape((NX, NY, NZ, 6, F)).astype(jnp.int32),
    }


def from_lower(array, axis):
    count = array.shape[axis]
    kept = lax.slice_in_dim(array, 0, count - 1, axis=axis)
    zeros = jnp.zeros_like(lax.slice_in_dim(array, 0, 1, axis=axis))
    return jnp.concatenate([zeros, kept], axis=axis)

def from_upper(array, axis):
    count = array.shape[axis]
    kept = lax.slice_in_dim(array, 1, count, axis=axis)
    zeros = jnp.zeros_like(lax.slice_in_dim(array, 0, 1, axis=axis))
    return jnp.concatenate([kept, zeros], axis=axis)

def local_products(lowered, operator):
    shape = lowered.shape
    flat_rows = lowered.reshape((-1,) + shape[3:])
    flat_ops = operator.reshape((-1,) + operator.shape[3:])

    def single(pieces):
        return jnp.dot(pieces[0], pieces[1], preferred_element_type=jnp.float32).astype(jnp.bfloat16)
    return lax.map(single, (flat_rows, flat_ops)).reshape(shape)

def reference(seed_cotangent, trace_operator, face_matrices, saved_traces, edge_flags, node_map):
    width = face_matrices.shape[-1]
    span = 6 * width
    sweeps = saved_traces.shape[3]
    columns = seed_cotangent.shape[3]
    seeded = seed_cotangent.astype(jnp.float32)
    state = seeded
    total = jnp.zeros(face_matrices.shape, jnp.float32)
    for sweep in range(sweeps):
        hidden = local_products(state.astype(jnp.bfloat16), trace_operator)
        own = jnp.stack([hidden[..., number * width:(number + 1) * width] for number in range(6)], axis=3)
        received = jnp.stack([from_lower(own[:, :, :, 1], 0), from_upper(own[:, :, :, 0], 0), from_lower(own[:, :, :, 3], 1), from_upper(own[:, :, :, 2], 1), from_lower(own[:, :, :, 5], 2), from_upper(own[:, :, :, 4], 2)], axis=3)
        mapped = jnp.take_along_axis(received, node_map[:, :, :, :, None, :], axis=5)
        chosen = jnp.where(edge_flags[..., None, None] == 1, own, mapped)
        fresh = jnp.einsum('xyzkcf,xyzkfg->xyzkcg', chosen.astype(jnp.float32), face_matrices.astype(jnp.float32))
        state = jnp.concatenate([fresh[:, :, :, number] for number in range(6)] + [hidden[..., span:].astype(jnp.float32)], axis=-1) + seeded
        stored = saved_traces[:, :, :, sweeps - 1 - sweep]
        stored_faces = jnp.stack([stored[..., number * width:(number + 1) * width] for number in range(6)], axis=3)
        total = total + jnp.einsum('xyzkcf,xyzkcg->xyzkfg', chosen.astype(jnp.float32), stored_faces.astype(jnp.float32))
    adjoint_traces = state.astype(jnp.bfloat16)
    face_gradient = (total * (1.0 / jnp.sqrt(jnp.float32(columns)))).astype(jnp.bfloat16)
    return (adjoint_traces, face_gradient)
```

```python
import functools
import math

import jax
import jax.numpy as jnp
from jax import lax
from jax.experimental import pallas as pl
from jax.experimental.pallas import tpu as pltpu
from jax.sharding import PartitionSpec as P

AXES = ("gx", "gy", "gz")
ORDER = (1, 0, 4, 5, 3, 2)
VMEM = pl.BlockSpec(memory_space=pltpu.VMEM)
SMEM = pl.BlockSpec(memory_space=pltpu.SMEM)
HBM = pl.BlockSpec(memory_space=pltpu.HBM)
BF16 = jnp.bfloat16
F32 = jnp.float32
PARAMS = pltpu.CompilerParams(vmem_limit_bytes=16 * 1024 * 1024)


def vmem(array):
    return pltpu.with_memory_space_constraint(array, pltpu.VMEM)


def swap(block, axis, shift):
    count = lax.axis_size(axis)
    pairs = []
    for i in range(count):
        up = (i + shift) % 2 == 0
        pairs.append((i, (i + 1) % count if up else (i - 1) % count))
    return lax.ppermute(block, axis, pairs)


def is_even(axis):
    return lax.rem(lax.axis_index(axis), 2) == 0


def store_faces(hidden, width, sends):
    for a, axis in enumerate(AXES):
        even = is_even(axis)
        low = hidden[:, 2 * a * width : (2 * a + 1) * width]
        high = hidden[:, (2 * a + 1) * width : (2 * a + 2) * width]
        sends[2 * a][...] = jnp.where(even, high, low)
        sends[2 * a + 1][...] = jnp.where(even, low, high)


def chosen_faces(sends, recvs, flags):
    faces = []
    for a, axis in enumerate(AXES):
        even = is_even(axis)
        place = lax.axis_index(axis)
        last = lax.axis_size(axis) - 1
        for side in range(2):
            first = even if side == 1 else jnp.logical_not(even)
            own = jnp.where(first, sends[2 * a][...], sends[2 * a + 1][...])
            got = jnp.where(first, recvs[2 * a][...], recvs[2 * a + 1][...])
            outer = place == (0 if side == 0 else last)
            got = jnp.where(outer, jnp.zeros_like(got), got)
            faces.append(jnp.where(flags[2 * a + side] == 1, own, got))
    return faces


def selector(flags, node_map, k, width):
    rows = lax.broadcasted_iota(jnp.int32, (width, width), 0)
    columns = lax.broadcasted_iota(jnp.int32, (1, width), 1)
    target = jnp.where(flags[k] == 1, columns, node_map[k : k + 1, :])
    return jnp.where(rows == target, 1.0, 0.0).astype(BF16)


def fill_state(state, faces, weights, seed, tail, width):
    trace = seed.shape[1]
    edge = tail.shape[1]
    state[:, trace - edge :] = tail[...].astype(F32)
    for k in range(6):
        fresh = jnp.dot(faces[k], weights[k], preferred_element_type=F32)
        state[:, k * width : (k + 1) * width] = fresh
    return (state[...] + seed[...].astype(F32)).astype(BF16)


def first_kernel(chunk, seed, operator_hbm, *refs):
    sends, (tail, operator), (hidden, sems) = refs[:6], refs[6:8], refs[8:]
    trace = seed.shape[1]
    width = sends[0].shape[1]
    copies = []
    for j in range(trace // chunk):
        span = pl.ds(j * chunk, chunk)
        copy = pltpu.make_async_copy(operator_hbm.at[:, span], operator.at[:, span], sems.at[j])
        copy.start()
        copies.append(copy)
    for j, copy in enumerate(copies):
        copy.wait()
        span = pl.ds(j * chunk, chunk)
        hidden[:, span] = jnp.dot(seed[...], operator[:, span], preferred_element_type=F32).astype(BF16)
    store_faces(hidden, width, sends)
    tail[...] = hidden[:, trace - tail.shape[1] :]


def middle_kernel(chunk, flags, weights, seed, operator, old_tail, *refs):
    sends, recvs, outs, tail, chosen, state, hidden = (
        refs[:6], refs[6:12], refs[12:18], refs[18], refs[19], refs[20], refs[21],
    )
    trace = seed.shape[1]
    width = sends[0].shape[1]
    faces = chosen_faces(sends, recvs, flags)
    for k in range(6):
        chosen[k] = faces[k]
    lowered = fill_state(state, faces, weights, seed, old_tail, width)
    for j in range(trace // chunk):
        span = pl.ds(j * chunk, chunk)
        hidden[:, span] = jnp.dot(lowered, operator[:, span], preferred_element_type=F32).astype(BF16)
    store_faces(hidden, width, outs)
    tail[...] = hidden[:, trace - tail.shape[1] :]


def place_kernel(flags, node_map, matrices, saved, weights, choosers, stored):
    sweeps = saved.shape[0]
    columns = saved.shape[1]
    width = matrices.shape[-1]
    for k in range(6):
        choosers[k] = selector(flags, node_map, k, width)
        weights[k] = jnp.dot(choosers[k], matrices[k], preferred_element_type=F32).astype(BF16)
        for sweep in range(sweeps):
            rows = slice((sweeps - 1 - sweep) * columns, (sweeps - sweep) * columns)
            stored[k, rows, :] = saved[sweep, :, k * width : (k + 1) * width]


def transposed_product(left, right):
    return lax.dot_general(left, right, (((0,), (0,)), ((), ())), preferred_element_type=F32)


def gradient_kernel(chosen_a, chosen_b, choosers, stored, total, both):
    columns = chosen_a.shape[1]
    for k in range(6):
        both[:columns] = chosen_a[k]
        both[columns:] = chosen_b[k]
        mapped = jnp.dot(both[...], choosers[k], preferred_element_type=F32).astype(BF16)
        total[k] = transposed_product(mapped, stored[k, : 2 * columns, :])


def last_kernel(flags, weights, seed, choosers, stored, old_tail, total, *refs):
    sends, recvs, adjoint_hbm, gradient_hbm, state, adjoint, gradient, sems = (
        refs[:6], refs[6:12], refs[12], refs[13], refs[14], refs[15], refs[16], refs[17],
    )
    columns = seed.shape[0]
    width = sends[0].shape[1]
    faces = chosen_faces(sends, recvs, flags)
    adjoint[...] = fill_state(state, faces, weights, seed, old_tail, width)
    copies = [pltpu.make_async_copy(adjoint, adjoint_hbm, sems.at[6])]
    copies[0].start()
    scale = 1.0 / math.sqrt(columns)
    for k in range(6):
        mapped = jnp.dot(faces[k], choosers[k], preferred_element_type=F32).astype(BF16)
        part = total[k] + transposed_product(mapped, stored[k, 2 * columns :, :])
        gradient[k] = (part * scale).astype(BF16)
        copies.append(pltpu.make_async_copy(gradient.at[k], gradient_hbm.at[k], sems.at[k]))
        copies[-1].start()
    for copy in copies:
        copy.wait()


def exchange(sends):
    recvs = [None] * 6
    for slot in ORDER:
        recvs[slot] = swap(sends[slot], AXES[slot // 2], slot % 2)
    return recvs


def local(seed_cotangent, trace_operator, face_matrices, saved_traces, edge_flags, node_map):
    seed = vmem(seed_cotangent[0, 0, 0])
    operator_hbm = trace_operator[0, 0, 0]
    matrices = vmem(face_matrices[0, 0, 0])
    saved = vmem(saved_traces[0, 0, 0])
    flags = edge_flags[0, 0, 0]
    mapping = vmem(node_map[0, 0, 0])
    columns, trace = seed.shape
    width = matrices.shape[-1]
    sweeps = saved.shape[0]
    edge = 128
    chunk = 512
    face = pltpu.VMEM((columns, width), BF16)
    tail_shape = pltpu.VMEM((columns, edge), BF16)
    block = (6, width, width)
    row = pltpu.VMEM((columns, trace), F32)

    def cost(flops, read):
        return pl.CostEstimate(flops=int(flops), bytes_accessed=int(read), transcendentals=0)

    big = 2 * columns * trace * trace
    small = 2 * 6 * columns * width * width
    results = pl.pallas_call(
        functools.partial(first_kernel, chunk),
        out_shape=[face] * 6 + [tail_shape, pltpu.VMEM((trace, trace), BF16)],
        in_specs=[VMEM, HBM],
        out_specs=[VMEM] * 8,
        scratch_shapes=[pltpu.VMEM((columns, trace), BF16), pltpu.SemaphoreType.DMA((trace // chunk,))],
        compiler_params=PARAMS,
        cost_estimate=cost(big, 2 * trace * trace),
        name="first",
    )(seed, operator_hbm)
    sends, tail, operator = results[:6], results[6], results[7]
    weights, choosers, stored = pl.pallas_call(
        place_kernel,
        out_shape=[
            pltpu.VMEM(block, BF16),
            pltpu.VMEM(block, BF16),
            pltpu.VMEM((6, sweeps * columns, width), BF16),
        ],
        in_specs=[SMEM] + [VMEM] * 3,
        out_specs=[VMEM] * 3,
        compiler_params=PARAMS,
        cost_estimate=cost(12 * width**3, 0),
        name="place",
    )(flags, mapping, matrices, saved)
    weights, choosers, stored, operator = map(vmem, (weights, choosers, stored, operator))
    chosen = []
    for sweep in range(sweeps - 1):
        recvs = exchange(sends)
        results = pl.pallas_call(
            functools.partial(middle_kernel, chunk),
            out_shape=[face] * 6 + [tail_shape, pltpu.VMEM((6, columns, width), BF16)],
            in_specs=[SMEM] + [VMEM] * 16,
            out_specs=[VMEM] * 8,
            scratch_shapes=[row, pltpu.VMEM((columns, trace), BF16)],
            compiler_params=PARAMS,
            cost_estimate=cost(big + small, 0),
            name="middle",
        )(flags, weights, seed, operator, vmem(tail), *map(vmem, sends), *map(vmem, recvs))
        sends, tail = results[:6], results[6]
        chosen.append(vmem(results[7]))
    total = pl.pallas_call(
        gradient_kernel,
        out_shape=pltpu.VMEM(block, F32),
        in_specs=[VMEM] * 4,
        out_specs=VMEM,
        scratch_shapes=[pltpu.VMEM((2 * columns, width), BF16)],
        compiler_params=PARAMS,
        cost_estimate=cost(4 * small, 0),
        name="gradient",
    )(*chosen, choosers, stored)
    recvs = exchange(sends)
    adjoint, gradient = pl.pallas_call(
        last_kernel,
        out_shape=[
            jax.ShapeDtypeStruct((columns, trace), BF16),
            jax.ShapeDtypeStruct(block, BF16),
        ],
        in_specs=[SMEM] + [VMEM] * 18,
        out_specs=[HBM] * 2,
        scratch_shapes=[
            row,
            pltpu.VMEM((columns, trace), BF16),
            pltpu.VMEM(block, BF16),
            pltpu.SemaphoreType.DMA((7,)),
        ],
        compiler_params=PARAMS,
        cost_estimate=cost(3 * small, 0),
        name="last",
    )(flags, weights, seed, choosers, stored, vmem(tail), vmem(total), *map(vmem, sends), *map(vmem, recvs))
    return (adjoint[None, None, None], gradient[None, None, None])


def solution(mesh):
    return jax.shard_map(
        local,
        mesh=mesh,
        in_specs=(
            P("gx", "gy", "gz", None, None),
            P("gx", "gy", "gz", None, None),
            P("gx", "gy", "gz", None, None, None),
            P("gx", "gy", "gz", None, None, None),
            P("gx", "gy", "gz", None),
            P("gx", "gy", "gz", None, None),
        ),
        out_specs=(P("gx", "gy", "gz", None, None), P("gx", "gy", "gz", None, None, None)),
        check_vma=False,
    )
```

```python
import functools
import math

import jax
import jax.numpy as jnp
from jax import lax
from jax.experimental import pallas as pl
from jax.experimental.pallas import tpu as pltpu
from jax.sharding import PartitionSpec as P

AXES = ("gx", "gy", "gz")
ORDER = (1, 0, 4, 5, 3, 2)
VMEM = pl.BlockSpec(memory_space=pltpu.VMEM)
SMEM = pl.BlockSpec(memory_space=pltpu.SMEM)
HBM = pl.BlockSpec(memory_space=pltpu.HBM)
BF16 = jnp.bfloat16
F32 = jnp.float32
PARAMS = pltpu.CompilerParams(vmem_limit_bytes=16 * 1024 * 1024)


def hbm(array):
    return pltpu.with_memory_space_constraint(array, pltpu.HBM)


def vmem(array):
    return pltpu.with_memory_space_constraint(array, pltpu.VMEM)


def swap(block, axis, shift):
    count = lax.axis_size(axis)
    pairs = []
    for i in range(count):
        up = (i + shift) % 2 == 0
        pairs.append((i, (i + 1) % count if up else (i - 1) % count))
    return lax.ppermute(block, axis, pairs)


def is_even(axis):
    return lax.rem(lax.axis_index(axis), 2) == 0


def store_faces(hidden, width, axis_numbers, sends):
    for n, a in enumerate(axis_numbers):
        even = is_even(AXES[a])
        low = hidden[:, 2 * a * width : (2 * a + 1) * width]
        high = hidden[:, (2 * a + 1) * width : (2 * a + 2) * width]
        sends[2 * n][...] = jnp.where(even, high, low)
        sends[2 * n + 1][...] = jnp.where(even, low, high)


def chosen_faces(sends, recvs, flags):
    faces = []
    for a, axis in enumerate(AXES):
        even = is_even(axis)
        place = lax.axis_index(axis)
        last = lax.axis_size(axis) - 1
        for side in range(2):
            first = even if side == 1 else jnp.logical_not(even)
            own = jnp.where(first, sends[2 * a][...], sends[2 * a + 1][...])
            got = jnp.where(first, recvs[2 * a][...], recvs[2 * a + 1][...])
            outer = place == (0 if side == 0 else last)
            got = jnp.where(outer, jnp.zeros_like(got), got)
            faces.append(jnp.where(flags[2 * a + side] == 1, own, got))
    return faces


def selector(flags, node_map, k, width):
    rows = lax.broadcasted_iota(jnp.int32, (width, width), 0)
    columns = lax.broadcasted_iota(jnp.int32, (1, width), 1)
    target = jnp.where(flags[k] == 1, columns, node_map[k : k + 1, :])
    return jnp.where(rows == target, 1.0, 0.0).astype(BF16)


def fill_state(state, faces, weights, seed, tail, width):
    trace = seed.shape[1]
    edge = tail.shape[1]
    state[:, trace - edge :] = tail[...].astype(F32)
    for k in range(6):
        fresh = jnp.dot(faces[k], weights[k], preferred_element_type=F32)
        state[:, k * width : (k + 1) * width] = fresh
    return (state[...] + seed[...].astype(F32)).astype(BF16)


def first_kernel(chunk, seed_hbm, operator_hbm, send_a, send_b, joint, seed, operator, hidden, sems):
    width = send_a.shape[1]
    shared = joint.shape[1]
    head = operator.shape[1]
    copies = [pltpu.make_async_copy(seed_hbm, seed, sems.at[0])]
    for j in range(head // chunk):
        span = pl.ds(j * chunk, chunk)
        copies.append(
            pltpu.make_async_copy(operator_hbm.at[:, span], operator.at[:, span], sems.at[j + 1])
        )
    for copy in copies:
        copy.start()
    copies[0].wait()
    for j, copy in enumerate(copies[1:]):
        copy.wait()
        span = pl.ds(j * chunk, chunk)
        hidden[:, span] = jnp.dot(seed[...], operator[:, span], preferred_element_type=F32).astype(BF16)
    store_faces(hidden, width, (0,), (send_a, send_b))
    joint[...] = hidden[:, head - shared :]


def rest_kernel(chunk, head, state, operator, joint, *refs):
    sends, tail, hidden = refs[:4], refs[4], refs[5]
    width = sends[0].shape[1]
    trace = state.shape[1]
    hidden[:, head - joint.shape[1] : head] = joint[...]
    for start in range(head, trace, chunk):
        span = pl.ds(start, chunk)
        hidden[:, span] = jnp.dot(state[...], operator[:, span], preferred_element_type=F32).astype(BF16)
    store_faces(hidden, width, (1, 2), sends)
    tail[...] = hidden[:, trace - tail.shape[1] :]


def middle_kernel(chunk, head, flags, weights, seed, operator, *refs):
    refs = refs[7:13] + refs[:6] + refs[14:] + (refs[6],)
    tail = refs[-1]
    sends, recvs, outs, joint, chosen, lowered, state, hidden = (
        refs[:6], refs[6:12], refs[12:14], refs[14], refs[15], refs[16], refs[17], refs[18],
    )
    width = sends[0].shape[1]
    faces = chosen_faces(sends, by_slot(recvs), flags)
    for k in range(6):
        chosen[k] = faces[k]
    lowered[...] = fill_state(state, faces, weights, seed, tail, width)
    for start in range(0, head, chunk):
        span = pl.ds(start, chunk)
        hidden[:, span] = jnp.dot(lowered[...], operator[:, span], preferred_element_type=F32).astype(BF16)
    store_faces(hidden, width, (0,), outs)
    joint[...] = hidden[:, head - joint.shape[1] : head]


def place_kernel(flags, node_map, matrices, saved, weights, choosers, stored):
    sweeps = saved.shape[0]
    columns = saved.shape[1]
    width = matrices.shape[-1]
    for k in range(6):
        choosers[k] = selector(flags, node_map, k, width)
        weights[k] = jnp.dot(choosers[k], matrices[k], preferred_element_type=F32).astype(BF16)
        for sweep in range(sweeps):
            rows = slice((sweeps - 1 - sweep) * columns, (sweeps - sweep) * columns)
            stored[k, rows, :] = saved[sweep, :, k * width : (k + 1) * width]


def transposed_product(left, right):
    return lax.dot_general(left, right, (((0,), (0,)), ((), ())), preferred_element_type=F32)


def gradient_kernel(chosen_a, chosen_b, choosers, stored, total, both):
    columns = chosen_a.shape[1]
    for k in range(6):
        both[:columns] = chosen_a[k]
        both[columns:] = chosen_b[k]
        mapped = jnp.dot(both[...], choosers[k], preferred_element_type=F32).astype(BF16)
        total[k] = transposed_product(mapped, stored[k, : 2 * columns, :])


def last_kernel(flags, weights, seed, choosers, stored, *refs):
    old_tail, total = refs[6:8]
    refs = refs[8:14] + refs[:6] + refs[15:]
    sends, recvs, adjoint_hbm, gradient_hbm, state, adjoint, gradient, sems = (
        refs[:6], refs[6:12], refs[12], refs[13], refs[14], refs[15], refs[16], refs[17],
    )
    columns = seed.shape[0]
    width = sends[0].shape[1]
    faces = chosen_faces(sends, by_slot(recvs), flags)
    adjoint[...] = fill_state(state, faces, weights, seed, old_tail, width)
    copies = [pltpu.make_async_copy(adjoint, adjoint_hbm, sems.at[6])]
    copies[0].start()
    scale = 1.0 / math.sqrt(columns)
    for k in range(6):
        mapped = jnp.dot(faces[k], choosers[k], preferred_element_type=F32).astype(BF16)
        part = total[k] + transposed_product(mapped, stored[k, 2 * columns :, :])
        gradient[k] = (part * scale).astype(BF16)
        copies.append(pltpu.make_async_copy(gradient.at[k], gradient_hbm.at[k], sems.at[k]))
        copies[-1].start()
    for copy in copies:
        copy.wait()


def exchange(sends, slots):
    return [vmem(swap(send, AXES[slot // 2], slot % 2)) for send, slot in zip(sends, slots)]


def by_slot(recvs):
    return [recvs[ORDER.index(slot)] for slot in range(6)]


def local(seed_cotangent, trace_operator, face_matrices, saved_traces, edge_flags, node_map):
    seed_hbm = hbm(seed_cotangent[0, 0, 0])
    operator_hbm = hbm(trace_operator[0, 0, 0])
    operator = vmem(trace_operator[0, 0, 0])
    matrices = vmem(face_matrices[0, 0, 0])
    saved = vmem(saved_traces[0, 0, 0])
    flags = edge_flags[0, 0, 0]
    mapping = vmem(node_map[0, 0, 0])
    columns, trace = seed_hbm.shape
    width = matrices.shape[-1]
    sweeps = saved.shape[0]
    edge = 128
    chunk = 256
    head = -(-2 * width // chunk) * chunk
    face = pltpu.VMEM((columns, width), BF16)
    tail_shape = pltpu.VMEM((columns, edge), BF16)
    block = (6, width, width)
    row = pltpu.VMEM((columns, trace), F32)

    def cost(flops, read):
        return pl.CostEstimate(flops=int(flops), bytes_accessed=int(read), transcendentals=0)

    big = 2 * columns * trace * trace
    small = 2 * 6 * columns * width * width
    def rest(state, joint):
        results = pl.pallas_call(
            functools.partial(rest_kernel, chunk, head),
            out_shape=[face] * 4 + [tail_shape],
            in_specs=[VMEM] * 3,
            out_specs=[VMEM] * 5,
            scratch_shapes=[lowered_scratch],
            compiler_params=PARAMS,
            cost_estimate=cost(big * (trace - head) // trace, 0),
            name="rest",
        )(vmem(state), operator, vmem(joint))
        return list(results[:4]), results[4]

    lowered_scratch = pltpu.VMEM((columns, trace), BF16)
    joint_shape = pltpu.VMEM((columns, head - 2 * width // 128 * 128), BF16)
    *sends, joint, seed = pl.pallas_call(
        functools.partial(first_kernel, chunk),
        out_shape=[face, face, joint_shape, pltpu.VMEM((columns, trace), BF16)],
        in_specs=[HBM] * 2,
        out_specs=[VMEM] * 4,
        scratch_shapes=[
            pltpu.VMEM((trace, head), BF16),
            pltpu.VMEM((columns, head), BF16),
            pltpu.SemaphoreType.DMA((head // chunk + 1,)),
        ],
        compiler_params=PARAMS,
        cost_estimate=cost(big * head // trace, 2 * trace * head),
        name="first",
    )(seed_hbm, operator_hbm)
    state = seed = vmem(seed)
    recvs = exchange([sends[slot] for slot in ORDER[:2]], ORDER[:2])
    others, tail = rest(seed, joint)
    sends = sends + others
    recvs = recvs + exchange([sends[slot] for slot in ORDER[2:]], ORDER[2:])
    weights, choosers, stored = pl.pallas_call(
        place_kernel,
        out_shape=[
            pltpu.VMEM(block, BF16),
            pltpu.VMEM(block, BF16),
            pltpu.VMEM((6, sweeps * columns, width), BF16),
        ],
        in_specs=[SMEM] + [VMEM] * 3,
        out_specs=[VMEM] * 3,
        compiler_params=PARAMS,
        cost_estimate=cost(12 * width**3, 0),
        name="place",
    )(flags, mapping, matrices, saved)
    weights, choosers, stored = map(vmem, (weights, choosers, stored))
    chosen = []
    for sweep in range(sweeps - 1):
        *sends, joint, picked, state = pl.pallas_call(
            functools.partial(middle_kernel, chunk, head),
            out_shape=[
                face,
                face,
                joint_shape,
                pltpu.VMEM((6, columns, width), BF16),
                pltpu.VMEM((columns, trace), BF16),
            ],
            in_specs=[SMEM] + [VMEM] * 17,
            out_specs=[VMEM] * 5,
            scratch_shapes=[row, pltpu.VMEM((columns, head), BF16)],
            compiler_params=PARAMS,
            cost_estimate=cost(big * head // trace + small, 0),
            name="middle",
        )(flags, weights, seed, operator, *recvs, vmem(tail), *map(vmem, sends), vmem(state))
        chosen.append(vmem(picked))
        recvs = exchange([sends[slot] for slot in ORDER[:2]], ORDER[:2])
        others, tail = rest(state, joint)
        sends = sends + others
        recvs = recvs + exchange([sends[slot] for slot in ORDER[2:]], ORDER[2:])
    total = pl.pallas_call(
        gradient_kernel,
        out_shape=pltpu.VMEM(block, F32),
        in_specs=[VMEM] * 4,
        out_specs=VMEM,
        scratch_shapes=[pltpu.VMEM((2 * columns, width), BF16)],
        compiler_params=PARAMS,
        cost_estimate=cost(4 * small, 0),
        name="gradient",
    )(*chosen, choosers, stored)
    adjoint, gradient = pl.pallas_call(
        last_kernel,
        out_shape=[
            jax.ShapeDtypeStruct((columns, trace), BF16),
            jax.ShapeDtypeStruct(block, BF16),
        ],
        in_specs=[SMEM] + [VMEM] * 19,
        out_specs=[HBM] * 2,
        scratch_shapes=[
            row,
            pltpu.VMEM((columns, trace), BF16),
            pltpu.VMEM(block, BF16),
            pltpu.SemaphoreType.DMA((7,)),
        ],
        compiler_params=PARAMS,
        cost_estimate=cost(3 * small, 0),
        name="last",
    )(flags, weights, seed, choosers, stored, *recvs, vmem(tail), vmem(total), *map(vmem, sends), vmem(state))
    return (adjoint[None, None, None], gradient[None, None, None])


def solution(mesh):
    return jax.shard_map(
        local,
        mesh=mesh,
        in_specs=(
            P("gx", "gy", "gz", None, None),
            P("gx", "gy", "gz", None, None),
            P("gx", "gy", "gz", None, None, None),
            P("gx", "gy", "gz", None, None, None),
            P("gx", "gy", "gz", None),
            P("gx", "gy", "gz", None, None),
        ),
        out_specs=(P("gx", "gy", "gz", None, None), P("gx", "gy", "gz", None, None, None)),
        check_vma=False,
    )
```
